32 devices in a mesh: mic: 4 (over z), tm: 8 (over y, x, core).
Axes of the slice: x: 2, y: 2, z: 4, core: 2. Of those that a mesh axis runs over, the one named last changes fastest.
Arguments:
- signal: float32 [4, 8192, 512], P('mic', 'tm'), may hold values from -6 to 6
- conv_weight: float32 [2, 3, 2, 512, 512], replicated, may hold values from -0.1875 to 0.1875
- conv_bias: float32 [2, 3, 512], replicated, may hold values from -3 to 3
- transform_in: float32 [2, 512, 512], replicated, may hold values from -0.25 to 0.25
- transform_mid: float32 [2, 512, 512], replicated, may hold values from -0.25 to 0.25
- transform_out: float32 [2, 1024, 512], replicated, may hold values from -0.1875 to 0.1875
- transform_offsets_bias: float32 [2, 3, 512], replicated, may hold values from -3 to 3
Outputs:
- separated: float32 [4, 8192, 512], P('mic', 'tm')
The draws below stay inside these ranges and needn't reach their ends.
All inputs are finite; a program needn't handle non-finite values.
Results may differ from the reference program's by a relative error of at most 0.0001.
Values sent between devices are 32-bit elements; how exact they have to be, the bound alone decides.
A program may use at most 128 MiB of HBM per device.

```python
import jax
import jax.numpy as jnp
from jax import lax

C = 512
SEPARATOR_BLOCKS = 2
LAYERS = 3
BASE_DILATION = 512
MICS = 4
FRAMES = 8192


def shard_levels(own_key, shape, shards, least, high):
    loudness = 1.0
    for position, parts in shards:
        heights = jax.random.uniform(jax.random.fold_in(jax.random.fold_in(own_key, 6), position), (parts,), jnp.float32, least / len(shards), high / len(shards))
        loudness = loudness * jnp.repeat(jnp.exp(heights), shape[position] // parts).reshape((-1,) + (1,) * (len(shape) - 1 - position))
    return loudness


def centred(own_key, shape, scale, bound, split=(), held_as=jnp.bfloat16):
    array = scale * jax.random.normal(own_key, shape, jnp.float32)
    if split:
        array = array * shard_levels(own_key, shape, split, -0.22, 0.18)
    return jnp.clip(array, -bound, bound).astype(held_as)


def setup_inputs(seed: int = 0) -> dict:
    key_of = jax.random.split(jax.random.key(seed), 8)
    return {
        "signal": centred(key_of[0], (MICS, FRAMES, C), 1.0, 6.0, ((0, 4), (1, 8)), jnp.float32),
        "conv_weight": centred(key_of[1], (SEPARATOR_BLOCKS, LAYERS, 2, C, C), (2 * C) ** -0.5, 0.1875, (), jnp.float32),
        "conv_bias": centred(key_of[2], (SEPARATOR_BLOCKS, LAYERS, C), 0.5, 3.0, (), jnp.float32),
        "transform_in": centred(key_of[3], (SEPARATOR_BLOCKS, C, C), C ** -0.5, 0.25, (), jnp.float32),
        "transform_mid": centred(key_of[4], (SEPARATOR_BLOCKS, C, C), C ** -0.5, 0.25, (), jnp.float32),
        "transform_out": centred(key_of[5], (SEPARATOR_BLOCKS, 2 * C, C), (2 * C) ** -0.5, 0.1875, (), jnp.float32),
        "transform_offsets_bias": centred(key_of[6], (SEPARATOR_BLOCKS, 3, C), 0.5, 3.0, (), jnp.float32),
    }


def product(left, right):
    return jnp.einsum("mtc,cd->mtd", left, right, precision=lax.Precision.HIGHEST)


def delay_frames(values, dilation_factor):
    padding_frames = jnp.zeros((values.shape[0], dilation_factor, values.shape[2]), jnp.float32)
    return jnp.concatenate([padding_frames, values[:, :values.shape[1] - dilation_factor]], axis=1)


def reference(signal, conv_weight, conv_bias, transform_in, transform_mid, transform_out, transform_offsets_bias):
    hidden_activations = signal
    for section_index in range(SEPARATOR_BLOCKS):
        for layer_position in range(LAYERS):
            dilation_factor = BASE_DILATION * 2 ** layer_position
            delayed = delay_frames(hidden_activations, dilation_factor)
            before_tanh = product(hidden_activations, conv_weight[section_index, layer_position, 0]) + product(delayed, conv_weight[section_index, layer_position, 1]) + conv_bias[section_index, layer_position]
            hidden_activations = hidden_activations + jnp.tanh(before_tanh)
        mapped = jnp.tanh(product(hidden_activations, transform_in[section_index]) + transform_offsets_bias[section_index, 0])
        channel_mean = jnp.sum(mapped, axis=0, keepdims=True) / jnp.float32(MICS)
        pooled = jnp.tanh(product(channel_mean, transform_mid[section_index]) + transform_offsets_bias[section_index, 1])
        mixing = product(mapped, transform_out[section_index, :C]) + product(pooled, transform_out[section_index, C:]) + transform_offsets_bias[section_index, 2]
        hidden_activations = hidden_activations + jnp.tanh(mixing)
    return hidden_activations
```

```python
import jax
import jax.numpy as jnp
from jax import lax
from jax.sharding import PartitionSpec as P

AXES = ("mic", "tm")


def matmul(left, right):
    return jnp.dot(left, right, precision=lax.Precision.HIGH, preferred_element_type=jnp.float32)


def delay(values, steps):
    padding = jnp.zeros(values.shape[:1] + (steps,) + values.shape[2:], values.dtype)
    return jnp.concatenate([padding, values[:, : values.shape[1] - steps]], axis=1)


def body(
    signal,
    conv_weight,
    conv_bias,
    transform_in,
    transform_mid,
    transform_out,
    transform_offsets_bias,
):
    _, frames, channels = signal.shape
    sections, layers = conv_weight.shape[:2]
    half = frames // 2
    mics = lax.axis_size("mic")
    chains = lax.all_to_all(
        signal[0].reshape(2, half, channels), AXES, split_axis=1, concat_axis=0, tiled=True
    )
    hidden = chains.reshape(mics, -1, chains.shape[1], channels)
    for s in range(sections):
        for l in range(layers):
            delayed = delay(hidden, 2**l)
            hidden = hidden + jnp.tanh(
                matmul(hidden, conv_weight[s, l, 0])
                + matmul(delayed, conv_weight[s, l, 1])
                + conv_bias[s, l]
            )
        mapped = jnp.tanh(matmul(hidden, transform_in[s]) + transform_offsets_bias[s, 0])
        average = jnp.sum(mapped, axis=0) / jnp.float32(mics)
        pooled = jnp.tanh(matmul(average, transform_mid[s]) + transform_offsets_bias[s, 1])
        mixing = (
            matmul(mapped, transform_out[s, :channels])
            + matmul(pooled, transform_out[s, channels:])
            + transform_offsets_bias[s, 2]
        )
        hidden = hidden + jnp.tanh(mixing)
    back = lax.all_to_all(
        hidden.reshape(chains.shape), AXES, split_axis=0, concat_axis=1, tiled=True
    )
    return back.reshape(1, frames, channels)


def solution(mesh):
    placed = (P("mic", "tm", None), P(), P(), P(), P(), P(), P())
    return jax.shard_map(
        body, mesh=mesh, in_specs=placed, out_specs=P("mic", "tm", None), check_vma=False
    )
```

```python
import functools

import jax
import jax.numpy as jnp
from jax import lax
from jax.experimental import pallas as pl
from jax.experimental.pallas import tpu as pltpu
from jax.sharding import PartitionSpec as P

AXES = ("mic", "tm")
ROWS = 8
MESH = pl.DeviceIdType.MESH


def matmul(left, right):
    return jnp.dot(left, right, precision=lax.Precision.HIGH, preferred_element_type=jnp.float32)


def delay(values, steps):
    padding = jnp.zeros(values.shape[:1] + (steps,) + values.shape[2:], values.dtype)
    return jnp.concatenate([padding, values[:, : values.shape[1] - steps]], axis=1)


def body(
    signal,
    conv_weight,
    conv_bias,
    transform_in,
    transform_mid,
    transform_out,
    transform_offsets_bias,
):
    _, frames, channels = signal.shape
    sections, layers = conv_weight.shape[:2]
    half = frames // 2
    mics = lax.axis_size("mic")
    chains = lax.all_to_all(
        signal[0].reshape(2, half, channels), AXES, split_axis=1, concat_axis=0, tiled=True
    )
    hidden = chains.reshape(mics, -1, chains.shape[1], channels)
    for s in range(sections):
        for l in range(layers):
            delayed = delay(hidden, 2**l)
            hidden = hidden + jnp.tanh(
                matmul(hidden, conv_weight[s, l, 0])
                + matmul(delayed, conv_weight[s, l, 1])
                + conv_bias[s, l]
            )
        mapped = jnp.tanh(matmul(hidden, transform_in[s]) + transform_offsets_bias[s, 0])
        average = jnp.sum(mapped, axis=0) / jnp.float32(mics)
        pooled = jnp.tanh(matmul(average, transform_mid[s]) + transform_offsets_bias[s, 1])
        mixing = (
            matmul(mapped, transform_out[s, :channels])
            + matmul(pooled, transform_out[s, channels:])
            + transform_offsets_bias[s, 2]
        )
        hidden = hidden + jnp.tanh(mixing)
    back = lax.all_to_all(
        hidden.reshape(chains.shape), AXES, split_axis=0, concat_axis=1, tiled=True
    )
    return back.reshape(1, frames, channels)


def split(values):
    high = values.astype(jnp.bfloat16)
    return high, (values - high.astype(jnp.float32)).astype(jnp.bfloat16)


def dot(left, right):
    return jnp.dot(left, right, preferred_element_type=jnp.float32)


def kernel(
    chunks,
    sections,
    layers,
    x_ref,
    conv_hbm,
    in_hbm,
    mid_hbm,
    out_hbm,
    conv_bias,
    offsets,
    y_ref,
    hidden,
    act_a,
    act_b,
    act_u,
    act_v,
    mixed,
    conv_f32,
    one_f32,
    conv_w,
    in_w,
    mid_w,
    out_w,
    send_sem,
    recv_sem,
    back_send_sem,
    back_recv_sem,
    weight_sem,
):
    mics, tms = lax.axis_size("mic"), lax.axis_size("tm")
    devices = mics * tms
    my_mic, my_tm = lax.axis_index("mic"), lax.axis_index("tm")
    me = my_mic * tms + my_tm
    share = chunks * ROWS
    channels = x_ref.shape[2]
    blocks = 2 * tms
    rows = blocks * mics * ROWS
    pad = act_a.shape[0] - rows

    order = sorted(range(mics), key=lambda j: -min(j, mics - j))

    def others(act):
        for jm in order:
            def one(jt, carry, jm=jm):
                act(lax.rem(my_mic + jm, mics), lax.rem(my_tm + jt, tms))
                return carry

            lax.fori_loop(1 if jm == 0 else 0, tms, one, 0)

    barrier = pltpu.get_barrier_semaphore()
    others(
        lambda m, t: pl.semaphore_signal(barrier, inc=1, device_id=(m, t), device_id_type=MESH)
    )
    pl.semaphore_wait(barrier, devices - 1)

    def residues(owner, k):
        return pl.ds(pl.multiple_of(owner * share + k * ROWS, ROWS), ROWS)

    for k in range(chunks):
        def send(m, t, k=k):
            pltpu.make_async_remote_copy(
                src_ref=x_ref.at[:, residues(m * tms + t, k)],
                dst_ref=hidden.at[k, pl.ds(2 * my_tm, 2), my_mic],
                send_sem=send_sem,
                recv_sem=recv_sem.at[k],
                device_id=(m, t),
                device_id_type=MESH,
            ).start()

        others(send)
        pltpu.make_async_copy(
            x_ref.at[:, residues(me, k)],
            hidden.at[k, pl.ds(2 * my_tm, 2), my_mic],
            recv_sem.at[k],
        ).start()

    conv_copy = pltpu.make_async_copy(conv_hbm, conv_f32, weight_sem.at[0])
    conv_copy.start()
    loads = []
    first = 0
    for n, source in enumerate((in_hbm, mid_hbm, out_hbm)):
        count = source.shape[0]
        copy = pltpu.make_async_copy(source, one_f32.at[pl.ds(first, count)], weight_sem.at[1 + n])
        copy.start()
        loads.append((copy, first, count))
        first += count
    act_a[pl.ds(0, pad), :] = jnp.zeros((pad, 2 * channels), jnp.bfloat16)
    act_b[pl.ds(0, pad), :] = jnp.zeros((pad, 2 * channels), jnp.bfloat16)

    step = 64

    def split_into(source, index, target, place, high_row, low_row):
        def part(i, carry):
            at = pl.multiple_of(i * step, step)
            high, low = split(source[index, pl.ds(at, step), :])
            target[place, pl.ds(pl.multiple_of(high_row + at, step), step), :] = high
            target[place, pl.ds(pl.multiple_of(low_row + at, step), step), :] = low
            return carry

        lax.fori_loop(0, channels // step, part, 0)

    conv_copy.wait()

    def conv_split(n, carry):
        for tap in range(2):
            split_into(conv_f32, 2 * n + tap, conv_w, n, tap * channels, (2 + tap) * channels)
        return carry

    lax.fori_loop(0, sections * layers, conv_split, 0)
    for (copy, first, count), target in zip(loads, (in_w, mid_w, out_w)):
        copy.wait()

        def other_split(n, carry, first=first, target=target):
            split_into(one_f32, first + n, target, n, 0, channels)
            return carry

        lax.fori_loop(0, count, other_split, 0)

    width = min(channels, 256)
    body = pl.ds(pad, rows)

    def product(act, part, weight, n, cols):
        high = act[part, pl.ds(0, channels)]
        low = act[part, pl.ds(channels, channels)]
        return dot(jnp.concatenate([high, high], axis=1), weight[n, :, cols]) + dot(
            low, weight[n, pl.ds(0, channels), cols]
        )

    def store(act, part, values, at):
        high, low = split(values)
        act[part, pl.ds(at, width)] = high
        act[part, pl.ds(channels + at, width)] = low

    def chunk(k, carry):
        pltpu.make_async_copy(hidden.at[k], hidden.at[k], recv_sem.at[k]).wait()
        for at in range(0, channels, width):
            now = hidden[k, :, :, :, pl.ds(at, width)].reshape(rows, width)
            store(act_a, body, now, at)

        def section(s, carry):
            here, there = act_a, act_b
            for l in range(layers):
                late = pl.ds(pad - 2**l * mics * ROWS, rows)
                n = s * layers + l
                for at in range(0, channels, width):
                    cols = pl.ds(at, width)
                    high = here[body, pl.ds(0, channels)]
                    late_high = here[late, pl.ds(0, channels)]
                    low = here[body, pl.ds(channels, channels)]
                    late_low = here[late, pl.ds(channels, channels)]
                    total = dot(
                        jnp.concatenate([high, late_high, high, late_high], axis=1),
                        conv_w[n, :, cols],
                    ) + dot(
                        jnp.concatenate([low, late_low], axis=1),
                        conv_w[n, pl.ds(0, 2 * channels), cols],
                    )
                    new = hidden[k, :, :, :, cols].reshape(rows, width) + jnp.tanh(
                        total + conv_bias[n, :, cols]
                    )
                    hidden[k, :, :, :, cols] = new.reshape(blocks, mics, ROWS, width)
                    store(there, body, new, at)
                here, there = there, here
            every = pl.ds(0, blocks * ROWS)
            for at in range(0, channels, width):
                cols = pl.ds(at, width)
                mapped = jnp.tanh(product(here, body, in_w, s, cols) + offsets[3 * s, :, cols])
                store(act_u, pl.ds(0, rows), mapped, at)
                average = jnp.sum(
                    mapped.reshape(blocks, mics, ROWS, width), axis=1
                ) / jnp.float32(mics)
                store(act_v, every, average.reshape(blocks * ROWS, width), at)
            for at in range(0, channels, width):
                cols = pl.ds(at, width)
                pooled = jnp.tanh(
                    product(act_v, every, mid_w, s, cols) + offsets[3 * s + 1, :, cols]
                )
                store(mixed, every, pooled, at)
            for at in range(0, channels, width):
                cols = pl.ds(at, width)
                shared = product(mixed, every, out_w, 2 * s + 1, cols) + offsets[3 * s + 2, :, cols]
                mixing = product(act_u, pl.ds(0, rows), out_w, 2 * s, cols).reshape(
                    blocks, mics, ROWS, width
                ) + shared.reshape(blocks, 1, ROWS, width)
                new = hidden[k, :, :, :, cols] + jnp.tanh(mixing)
                hidden[k, :, :, :, cols] = new
                store(act_a, body, new.reshape(rows, width), at)
            return carry

        lax.fori_loop(0, sections, section, 0)

        def send_back(m, t):
            pltpu.make_async_remote_copy(
                src_ref=hidden.at[k, pl.ds(2 * t, 2), m],
                dst_ref=y_ref.at[:, residues(me, k)],
                send_sem=back_send_sem,
                recv_sem=back_recv_sem,
                device_id=(m, t),
                device_id_type=MESH,
            ).start()

        others(send_back)
        pltpu.make_async_copy(
            hidden.at[k, pl.ds(2 * my_tm, 2), my_mic],
            y_ref.at[:, residues(me, k)],
            back_recv_sem,
        ).start()
        return carry

    lax.fori_loop(0, chunks, chunk, 0)

    sent = x_ref.at[:, pl.ds(0, (devices - 1) * share)]
    pltpu.make_async_copy(sent, sent, send_sem).wait()
    pltpu.make_async_copy(sent, sent, back_send_sem).wait()
    pltpu.make_async_copy(y_ref, y_ref, back_recv_sem).wait()


def fused(
    mics,
    tms,
    signal,
    conv_weight,
    conv_bias,
    transform_in,
    transform_mid,
    transform_out,
    transform_offsets_bias,
):
    _, frames, channels = signal.shape
    sections, layers = conv_weight.shape[:2]
    half = frames // 2
    chunks = half // (mics * tms) // ROWS
    blocks = 2 * tms
    rows = blocks * mics * ROWS
    pad = 2 ** (layers - 1) * mics * ROWS
    bf16, f32 = jnp.bfloat16, jnp.float32
    anywhere = pl.BlockSpec(memory_space=pl.ANY)
    vmem = pl.BlockSpec(memory_space=pltpu.VMEM)
    out = pl.pallas_call(
        functools.partial(kernel, chunks, sections, layers),
        out_shape=jax.ShapeDtypeStruct((2, half, channels), f32),
        in_specs=[anywhere] * 5 + [vmem] * 2,
        out_specs=anywhere,
        scratch_shapes=[
            pltpu.VMEM((chunks, blocks, mics, ROWS, channels), f32),
            pltpu.VMEM((pad + rows, 2 * channels), bf16),
            pltpu.VMEM((pad + rows, 2 * channels), bf16),
            pltpu.VMEM((rows, 2 * channels), bf16),
            pltpu.VMEM((blocks * ROWS, 2 * channels), bf16),
            pltpu.VMEM((blocks * ROWS, 2 * channels), bf16),
            pltpu.VMEM((sections * layers * 2, channels, channels), f32),
            pltpu.VMEM((sections * 4, channels, channels), f32),
            pltpu.VMEM((sections * layers, 4 * channels, channels), bf16),
            pltpu.VMEM((sections, 2 * channels, channels), bf16),
            pltpu.VMEM((sections, 2 * channels, channels), bf16),
            pltpu.VMEM((sections * 2, 2 * channels, channels), bf16),
            pltpu.SemaphoreType.DMA,
            pltpu.SemaphoreType.DMA((chunks,)),
            pltpu.SemaphoreType.DMA,
            pltpu.SemaphoreType.DMA,
            pltpu.SemaphoreType.DMA((4,)),
        ],
        compiler_params=pltpu.CompilerParams(
            collective_id=0, has_side_effects=True, vmem_limit_bytes=60 * 1024 * 1024
        ),
        name="sections",
    )(
        signal.reshape(2, half, channels),
        conv_weight.reshape(-1, channels, channels),
        transform_in,
        transform_mid,
        transform_out.reshape(-1, channels, channels),
        conv_bias.reshape(-1, 1, channels),
        transform_offsets_bias.reshape(-1, 1, channels),
    )
    return out.reshape(1, frames, channels)


def solution(mesh):
    mics, tms = mesh.shape["mic"], mesh.shape["tm"]

    def run(signal, *parameters):
        half = signal.shape[1] // 2
        if half % (mics * tms * ROWS) == 0 and mics % 2 == 0:
            return fused(mics, tms, signal, *parameters)
        return body(signal, *parameters)

    placed = (P("mic", "tm", None), P(), P(), P(), P(), P(), P())
    return jax.shard_map(
        run, mesh=mesh, in_specs=placed, out_specs=P("mic", "tm", None), check_vma=False
    )
```

```python
import functools

import jax
import jax.numpy as jnp
from jax import lax
from jax.experimental import pallas as pl
from jax.experimental.pallas import tpu as pltpu
from jax.sharding import PartitionSpec as P

AXES = ("mic", "tm")
ROWS = 8
MESH = pl.DeviceIdType.MESH


def matmul(left, right):
    return jnp.dot(left, right, precision=lax.Precision.HIGH, preferred_element_type=jnp.float32)


def delay(values, steps):
    padding = jnp.zeros(values.shape[:1] + (steps,) + values.shape[2:], values.dtype)
    return jnp.concatenate([padding, values[:, : values.shape[1] - steps]], axis=1)


def body(
    signal,
    conv_weight,
    conv_bias,
    transform_in,
    transform_mid,
    transform_out,
    transform_offsets_bias,
):
    _, frames, channels = signal.shape
    sections, layers = conv_weight.shape[:2]
    half = frames // 2
    mics = lax.axis_size("mic")
    chains = lax.all_to_all(
        signal[0].reshape(2, half, channels), AXES, split_axis=1, concat_axis=0, tiled=True
    )
    hidden = chains.reshape(mics, -1, chains.shape[1], channels)
    for s in range(sections):
        for l in range(layers):
            delayed = delay(hidden, 2**l)
            hidden = hidden + jnp.tanh(
                matmul(hidden, conv_weight[s, l, 0])
                + matmul(delayed, conv_weight[s, l, 1])
                + conv_bias[s, l]
            )
        mapped = jnp.tanh(matmul(hidden, transform_in[s]) + transform_offsets_bias[s, 0])
        average = jnp.sum(mapped, axis=0) / jnp.float32(mics)
        pooled = jnp.tanh(matmul(average, transform_mid[s]) + transform_offsets_bias[s, 1])
        mixing = (
            matmul(mapped, transform_out[s, :channels])
            + matmul(pooled, transform_out[s, channels:])
            + transform_offsets_bias[s, 2]
        )
        hidden = hidden + jnp.tanh(mixing)
    back = lax.all_to_all(
        hidden.reshape(chains.shape), AXES, split_axis=0, concat_axis=1, tiled=True
    )
    return back.reshape(1, frames, channels)


def split(values):
    high = values.astype(jnp.bfloat16)
    return high, (values - high.astype(jnp.float32)).astype(jnp.bfloat16)


def dot(left, right):
    return jnp.dot(left, right, preferred_element_type=jnp.float32)


def kernel(
    chunks,
    sections,
    layers,
    x_ref,
    conv_hbm,
    in_hbm,
    mid_hbm,
    out_hbm,
    conv_bias_hbm,
    offsets_hbm,
    y_ref,
    hidden,
    act_a,
    act_b,
    act_u,
    act_v,
    mixed,
    conv_f32,
    one_f32,
    conv_w,
    in_w,
    mid_w,
    out_w,
    conv_bias,
    offsets,
    send_sem,
    recv_sem,
    back_send_sem,
    back_recv_sem,
    weight_sem,
):
    mics, tms = lax.axis_size("mic"), lax.axis_size("tm")
    devices = mics * tms
    my_mic, my_tm = lax.axis_index("mic"), lax.axis_index("tm")
    me = my_mic * tms + my_tm
    share = chunks * ROWS
    channels = x_ref.shape[2]
    blocks = 2 * tms
    rows = blocks * mics * ROWS
    pad = act_a.shape[0] - rows

    order = sorted(range(mics), key=lambda j: -min(j, mics - j))

    def others(act):
        for jm in order:
            def one(jt, carry, jm=jm):
                act(lax.rem(my_mic + jm, mics), lax.rem(my_tm + jt, tms))
                return carry

            lax.fori_loop(1 if jm == 0 else 0, tms, one, 0)

    bias_copies = [
        pltpu.make_async_copy(conv_bias_hbm, conv_bias, weight_sem.at[4]),
        pltpu.make_async_copy(offsets_hbm, offsets, weight_sem.at[5]),
    ]
    for copy in bias_copies:
        copy.start()
    barrier = pltpu.get_barrier_semaphore()
    others(
        lambda m, t: pl.semaphore_signal(barrier, inc=1, device_id=(m, t), device_id_type=MESH)
    )
    pl.semaphore_wait(barrier, devices - 1)

    def residues(owner, k):
        return pl.ds(pl.multiple_of(owner * share + k * ROWS, ROWS), ROWS)

    for k in range(chunks):
        def send(m, t, k=k):
            pltpu.make_async_remote_copy(
                src_ref=x_ref.at[:, residues(m * tms + t, k)],
                dst_ref=hidden.at[k, pl.ds(2 * my_tm, 2), my_mic],
                send_sem=send_sem,
                recv_sem=recv_sem.at[k],
                device_id=(m, t),
                device_id_type=MESH,
            ).start()

        others(send)
        pltpu.make_async_copy(
            x_ref.at[:, residues(me, k)],
            hidden.at[k, pl.ds(2 * my_tm, 2), my_mic],
            recv_sem.at[k],
        ).start()

    conv_copy = pltpu.make_async_copy(conv_hbm, conv_f32, weight_sem.at[0])
    conv_copy.start()
    loads = []
    first = 0
    for n, source in enumerate((in_hbm, mid_hbm, out_hbm)):
        count = source.shape[0]
        copy = pltpu.make_async_copy(source, one_f32.at[pl.ds(first, count)], weight_sem.at[1 + n])
        copy.start()
        loads.append((copy, first, count))
        first += count
    act_a[pl.ds(0, pad), :] = jnp.zeros((pad, 2 * channels), jnp.bfloat16)
    act_b[pl.ds(0, pad), :] = jnp.zeros((pad, 2 * channels), jnp.bfloat16)

    step = 64

    def split_into(source, index, target, place, high_row, low_row):
        def part(i, carry):
            at = pl.multiple_of(i * step, step)
            high, low = split(source[index, pl.ds(at, step), :])
            target[place, pl.ds(pl.multiple_of(high_row + at, step), step), :] = high
            target[place, pl.ds(pl.multiple_of(low_row + at, step), step), :] = low
            return carry

        lax.fori_loop(0, channels // step, part, 0)

    for copy in bias_copies:
        copy.wait()
    conv_copy.wait()

    def conv_split(n, carry):
        for tap in range(2):
            split_into(conv_f32, 2 * n + tap, conv_w, n, tap * channels, (2 + tap) * channels)
        return carry

    lax.fori_loop(0, sections * layers, conv_split, 0)
    for (copy, first, count), target in zip(loads, (in_w, mid_w, out_w)):
        copy.wait()

        def other_split(n, carry, first=first, target=target):
            split_into(one_f32, first + n, target, n, 0, channels)
            return carry

        lax.fori_loop(0, count, other_split, 0)

    width = channels
    body = pl.ds(pad, rows)

    def product(act, part, weight, n, cols):
        high = act[part, pl.ds(0, channels)]
        low = act[part, pl.ds(channels, channels)]
        return dot(jnp.concatenate([high, high], axis=1), weight[n, :, cols]) + dot(
            low, weight[n, pl.ds(0, channels), cols]
        )

    def store(act, part, values, at):
        high, low = split(values)
        act[part, pl.ds(at, width)] = high
        act[part, pl.ds(channels + at, width)] = low

    def chunk(k, carry):
        pltpu.make_async_copy(hidden.at[k], hidden.at[k], recv_sem.at[k]).wait()
        for at in range(0, channels, width):
            now = hidden[k, :, :, :, pl.ds(at, width)].reshape(rows, width)
            store(act_a, body, now, at)

        def section(s, carry):
            here, there = act_a, act_b
            for l in range(layers):
                late = pl.ds(pad - 2**l * mics * ROWS, rows)
                n = s * layers + l
                for at in range(0, channels, width):
                    cols = pl.ds(at, width)
                    high = here[body, pl.ds(0, channels)]
                    late_high = here[late, pl.ds(0, channels)]
                    low = here[body, pl.ds(channels, channels)]
                    late_low = here[late, pl.ds(channels, channels)]
                    total = dot(
                        jnp.concatenate([high, late_high, high, late_high], axis=1),
                        conv_w[n, :, cols],
                    ) + dot(
                        jnp.concatenate([low, late_low], axis=1),
                        conv_w[n, pl.ds(0, 2 * channels), cols],
                    )
                    new = hidden[k, :, :, :, cols].reshape(rows, width) + jnp.tanh(
                        total + conv_bias[l, pl.ds(s, 1), cols]
                    )
                    hidden[k, :, :, :, cols] = new.reshape(blocks, mics, ROWS, width)
                    store(there, body, new, at)
                here, there = there, here
            every = pl.ds(0, blocks * ROWS)
            for at in range(0, channels, width):
                cols = pl.ds(at, width)
                mapped = jnp.tanh(product(here, body, in_w, s, cols) + offsets[0, pl.ds(s, 1), cols])
                store(act_u, pl.ds(0, rows), mapped, at)
                average = jnp.sum(
                    mapped.reshape(blocks, mics, ROWS, width), axis=1
                ) / jnp.float32(mics)
                store(act_v, every, average.reshape(blocks * ROWS, width), at)
            for at in range(0, channels, width):
                cols = pl.ds(at, width)
                pooled = jnp.tanh(
                    product(act_v, every, mid_w, s, cols) + offsets[1, pl.ds(s, 1), cols]
                )
                store(mixed, every, pooled, at)
            for at in range(0, channels, width):
                cols = pl.ds(at, width)
                shared = product(mixed, every, out_w, 2 * s + 1, cols) + offsets[2, pl.ds(s, 1), cols]
                mixing = product(act_u, pl.ds(0, rows), out_w, 2 * s, cols).reshape(
                    blocks, mics, ROWS, width
                ) + shared.reshape(blocks, 1, ROWS, width)
                new = hidden[k, :, :, :, cols] + jnp.tanh(mixing)
                hidden[k, :, :, :, cols] = new
                store(act_a, body, new.reshape(rows, width), at)
            return carry

        lax.fori_loop(0, sections, section, 0)

        def send_back(m, t):
            pltpu.make_async_remote_copy(
                src_ref=hidden.at[k, pl.ds(2 * t, 2), m],
                dst_ref=y_ref.at[:, residues(me, k)],
                send_sem=back_send_sem,
                recv_sem=back_recv_sem,
                device_id=(m, t),
                device_id_type=MESH,
            ).start()

        others(send_back)
        pltpu.make_async_copy(
            hidden.at[k, pl.ds(2 * my_tm, 2), my_mic],
            y_ref.at[:, residues(me, k)],
            back_recv_sem,
        ).start()
        return carry

    lax.fori_loop(0, chunks, chunk, 0)

    sent = x_ref.at[:, pl.ds(0, (devices - 1) * share)]
    pltpu.make_async_copy(sent, sent, send_sem).wait()
    pltpu.make_async_copy(sent, sent, back_send_sem).wait()
    pltpu.make_async_copy(y_ref, y_ref, back_recv_sem).wait()


def fused(
    mics,
    tms,
    signal,
    conv_weight,
    conv_bias,
    transform_in,
    transform_mid,
    transform_out,
    transform_offsets_bias,
):
    _, frames, channels = signal.shape
    sections, layers = conv_weight.shape[:2]
    half = frames // 2
    chunks = half // (mics * tms) // ROWS
    blocks = 2 * tms
    rows = blocks * mics * ROWS
    pad = 2 ** (layers - 1) * mics * ROWS
    bf16, f32 = jnp.bfloat16, jnp.float32
    anywhere = pl.BlockSpec(memory_space=pl.ANY)
    out = pl.pallas_call(
        functools.partial(kernel, chunks, sections, layers),
        out_shape=pltpu.VMEM((2, half, channels), f32),
        in_specs=[anywhere] * 7,
        out_specs=pl.BlockSpec(memory_space=pltpu.VMEM),
        scratch_shapes=[
            pltpu.VMEM((chunks, blocks, mics, ROWS, channels), f32),
            pltpu.VMEM((pad + rows, 2 * channels), bf16),
            pltpu.VMEM((pad + rows, 2 * channels), bf16),
            pltpu.VMEM((rows, 2 * channels), bf16),
            pltpu.VMEM((blocks * ROWS, 2 * channels), bf16),
            pltpu.VMEM((blocks * ROWS, 2 * channels), bf16),
            pltpu.VMEM((sections * layers * 2, channels, channels), f32),
            pltpu.VMEM((sections * 4, channels, channels), f32),
            pltpu.VMEM((sections * layers, 4 * channels, channels), bf16),
            pltpu.VMEM((sections, 2 * channels, channels), bf16),
            pltpu.VMEM((sections, 2 * channels, channels), bf16),
            pltpu.VMEM((sections * 2, 2 * channels, channels), bf16),
            pltpu.VMEM((layers, sections, channels), f32),
            pltpu.VMEM((3, sections, channels), f32),
            pltpu.SemaphoreType.DMA,
            pltpu.SemaphoreType.DMA((chunks,)),
            pltpu.SemaphoreType.DMA,
            pltpu.SemaphoreType.DMA,
            pltpu.SemaphoreType.DMA((6,)),
        ],
        compiler_params=pltpu.CompilerParams(
            collective_id=0, has_side_effects=True, vmem_limit_bytes=60 * 1024 * 1024
        ),
        name="sections",
    )(
        signal.reshape(2, half, channels),
        conv_weight.reshape(-1, channels, channels),
        transform_in,
        transform_mid,
        transform_out.reshape(-1, channels, channels),
        conv_bias.swapaxes(0, 1),
        transform_offsets_bias.swapaxes(0, 1),
    )
    return out.reshape(1, frames, channels)


def solution(mesh):
    mics, tms = mesh.shape["mic"], mesh.shape["tm"]

    def run(signal, *parameters):
        half = signal.shape[1] // 2
        if half % (mics * tms * ROWS) == 0 and mics % 2 == 0:
            return fused(mics, tms, signal, *parameters)
        return body(signal, *parameters)

    placed = (P("mic", "tm", None), P(), P(), P(), P(), P(), P())
    return jax.shard_map(
        run, mesh=mesh, in_specs=placed, out_specs=P("mic", "tm", None), check_vma=False
    )
```

```python
import functools

import jax
import jax.numpy as jnp
from jax import lax
from jax.experimental import pallas as pl
from jax.experimental.pallas import tpu as pltpu
from jax.sharding import PartitionSpec as P

AXES = ("mic", "tm")
ROWS = 8
MESH = pl.DeviceIdType.MESH


def matmul(left, right):
    return jnp.dot(left, right, precision=lax.Precision.HIGH, preferred_element_type=jnp.float32)


def delay(values, steps):
    padding = jnp.zeros(values.shape[:1] + (steps,) + values.shape[2:], values.dtype)
    return jnp.concatenate([padding, values[:, : values.shape[1] - steps]], axis=1)


def body(
    signal,
    conv_weight,
    conv_bias,
    transform_in,
    transform_mid,
    transform_out,
    transform_offsets_bias,
):
    _, frames, channels = signal.shape
    sections, layers = conv_weight.shape[:2]
    half = frames // 2
    mics = lax.axis_size("mic")
    chains = lax.all_to_all(
        signal[0].reshape(2, half, channels), AXES, split_axis=1, concat_axis=0, tiled=True
    )
    hidden = chains.reshape(mics, -1, chains.shape[1], channels)
    for s in range(sections):
        for l in range(layers):
            delayed = delay(hidden, 2**l)
            hidden = hidden + jnp.tanh(
                matmul(hidden, conv_weight[s, l, 0])
                + matmul(delayed, conv_weight[s, l, 1])
                + conv_bias[s, l]
            )
        mapped = jnp.tanh(matmul(hidden, transform_in[s]) + transform_offsets_bias[s, 0])
        average = jnp.sum(mapped, axis=0) / jnp.float32(mics)
        pooled = jnp.tanh(matmul(average, transform_mid[s]) + transform_offsets_bias[s, 1])
        mixing = (
            matmul(mapped, transform_out[s, :channels])
            + matmul(pooled, transform_out[s, channels:])
            + transform_offsets_bias[s, 2]
        )
        hidden = hidden + jnp.tanh(mixing)
    back = lax.all_to_all(
        hidden.reshape(chains.shape), AXES, split_axis=0, concat_axis=1, tiled=True
    )
    return back.reshape(1, frames, channels)


def split(values):
    high = values.astype(jnp.bfloat16)
    return high, (values - high.astype(jnp.float32)).astype(jnp.bfloat16)


def dot(left, right):
    return jnp.dot(left, right, preferred_element_type=jnp.float32)


def kernel(
    chunks,
    sections,
    layers,
    x_ref,
    conv_hbm,
    in_hbm,
    mid_hbm,
    out_hbm,
    conv_bias_hbm,
    offsets_hbm,
    y_ref,
    hidden,
    act_a,
    act_b,
    act_u,
    conv_f32,
    one_f32,
    conv_w,
    in_w,
    mid_w,
    out_w,
    conv_bias,
    offsets,
    send_sem,
    recv_sem,
    back_send_sem,
    back_recv_sem,
    weight_sem,
):
    mics, tms = lax.axis_size("mic"), lax.axis_size("tm")
    devices = mics * tms
    my_mic, my_tm = lax.axis_index("mic"), lax.axis_index("tm")
    me = my_mic * tms + my_tm
    share = chunks * ROWS
    channels = x_ref.shape[2]
    blocks = 2 * tms
    rows = blocks * (mics // 2) * ROWS
    pad = act_a.shape[1] - rows

    group = mics // 2
    near = my_mic // group
    far = 1 - near
    my_place = lax.rem(my_mic, group)

    def send_each(act, to_far=True, to_near=True):
        for j in range(group):
            place = lax.rem(my_place + j, group)

            def one(jt, carry, place=place):
                t = lax.rem(my_tm + jt, tms)
                if to_far:
                    act(far, place, t)
                if to_near:
                    act(near, place, t)
                return carry

            if j == 0 and to_far:
                act(far, place, my_tm)
            lax.fori_loop(1 if j == 0 else 0, tms, one, 0)

    bias_copies = [
        pltpu.make_async_copy(conv_bias_hbm, conv_bias, weight_sem.at[4]),
        pltpu.make_async_copy(offsets_hbm, offsets, weight_sem.at[5]),
    ]
    for copy in bias_copies:
        copy.start()
    barrier = pltpu.get_barrier_semaphore()
    send_each(
        lambda g, p, t: pl.semaphore_signal(
            barrier, inc=1, device_id=(g * group + p, t), device_id_type=MESH
        )
    )
    pl.semaphore_wait(barrier, devices - 1)

    def residues(owner, k):
        return pl.ds(pl.multiple_of(owner * share + k * ROWS, ROWS), ROWS)

    def send_chunk(k):
        def send(g, p, t):
            m = g * group + p
            pltpu.make_async_remote_copy(
                src_ref=x_ref.at[:, residues(m * tms + t, k)],
                dst_ref=hidden.at[k, near, pl.ds(2 * my_tm, 2), my_place],
                send_sem=send_sem,
                recv_sem=recv_sem.at[k, near],
                device_id=(m, t),
                device_id_type=MESH,
            ).start()

        send_each(send)
        pltpu.make_async_copy(
            x_ref.at[:, residues(me, k)],
            hidden.at[k, near, pl.ds(2 * my_tm, 2), my_place],
            recv_sem.at[k, near],
        ).start()

    send_chunk(0)

    conv_copy = pltpu.make_async_copy(conv_hbm, conv_f32, weight_sem.at[0])
    conv_copy.start()
    loads = []
    first = 0
    for n, source in enumerate((in_hbm, mid_hbm, out_hbm)):
        count = source.shape[0]
        copy = pltpu.make_async_copy(source, one_f32.at[pl.ds(first, count)], weight_sem.at[1 + n])
        copy.start()
        loads.append((copy, first, count))
        first += count
    for k in range(1, chunks):
        send_chunk(k)
    for g in range(2):
        act_a[g, pl.ds(0, pad), :] = jnp.zeros((pad, 2 * channels), jnp.bfloat16)
        act_b[g, pl.ds(0, pad), :] = jnp.zeros((pad, 2 * channels), jnp.bfloat16)

    step = 64

    def split_into(source, index, target, place, high_row, low_row):
        def part(i, carry):
            at = pl.multiple_of(i * step, step)
            high, low = split(source[index, pl.ds(at, step), :])
            target[place, pl.ds(pl.multiple_of(high_row + at, step), step), :] = high
            target[place, pl.ds(pl.multiple_of(low_row + at, step), step), :] = low
            return carry

        lax.fori_loop(0, channels // step, part, 0)

    for copy in bias_copies:
        copy.wait()
    conv_copy.wait()

    def conv_split(n, carry):
        for tap in range(2):
            split_into(conv_f32, 2 * n + tap, conv_w, n, tap * channels, (2 + tap) * channels)
        return carry

    lax.fori_loop(0, sections * layers, conv_split, 0)
    body = pl.ds(pad, rows)
    high_part, low_part = pl.ds(0, channels), pl.ds(channels, channels)
    shape = (blocks, group, ROWS, channels)

    def product(high, low, weight, n):
        return dot(jnp.concatenate([high, high], axis=1), weight[n]) + dot(
            low, weight[n, pl.ds(0, channels)]
        )

    def load(act, groups, part, columns):
        return jnp.concatenate([act[g, part, columns] for g in groups], axis=0)

    def store(act, g, part, values):
        high, low = split(values)
        act[g, part, high_part] = high
        act[g, part, low_part] = low

    def convolve(k, s, groups):
        for g in groups:
            store(act_a, g, body, hidden[k, g].reshape(rows, channels))
        here, there = act_a, act_b
        for l in range(layers):
            late = pl.ds(pad - 2**l * group * ROWS, rows)
            n = s * layers + l
            high = load(here, groups, body, high_part)
            late_high = load(here, groups, late, high_part)
            low = load(here, groups, body, low_part)
            late_low = load(here, groups, late, low_part)
            total = dot(
                jnp.concatenate([high, late_high, high, late_high], axis=1), conv_w[n]
            ) + dot(
                jnp.concatenate([low, late_low], axis=1),
                conv_w[n, pl.ds(0, 2 * channels)],
            )
            delta = jnp.tanh(total + conv_bias[l, pl.ds(s, 1), :])
            for i, g in enumerate(groups):
                new = hidden[k, g] + delta[i * rows : (i + 1) * rows].reshape(shape)
                hidden[k, g] = new
                if l < layers - 1:
                    store(there, g, body, new.reshape(rows, channels))
            here, there = there, here

    def connect(k, s, send):
        high, low = split(hidden[k].reshape(2 * rows, channels))
        mapped = jnp.tanh(product(high, low, in_w, s) + offsets[0, pl.ds(s, 1), :])
        for g in range(2):
            store(act_u, g, pl.ds(0, rows), mapped[g * rows : (g + 1) * rows])
        average = jnp.sum(mapped.reshape((2,) + shape), axis=(0, 2)) / jnp.float32(mics)
        high, low = split(average.reshape(blocks * ROWS, channels))
        pooled = jnp.tanh(product(high, low, mid_w, s) + offsets[1, pl.ds(s, 1), :])
        high, low = split(pooled)
        shared = product(high, low, out_w, 2 * s + 1) + offsets[2, pl.ds(s, 1), :]
        shared = shared.reshape(blocks, 1, ROWS, channels)
        for g in (far, near):
            mixing = product(
                act_u[g, :, high_part], act_u[g, :, low_part], out_w, 2 * s
            ).reshape(shape)
            hidden[k, g] = hidden[k, g] + jnp.tanh(mixing + shared)
            if send:
                send_back(k, g is far)

    def send_back(k, to_far):
        def send(g, p, t):
            pltpu.make_async_remote_copy(
                src_ref=hidden.at[k, g, pl.ds(2 * t, 2), p],
                dst_ref=y_ref.at[:, residues(me, k)],
                send_sem=back_send_sem,
                recv_sem=back_recv_sem,
                device_id=(g * group + p, t),
                device_id_type=MESH,
            ).start()

        send_each(send, to_far=to_far, to_near=not to_far)
        if not to_far:
            pltpu.make_async_copy(
                hidden.at[k, near, pl.ds(2 * my_tm, 2), my_place],
                y_ref.at[:, residues(me, k)],
                back_recv_sem,
            ).start()

    def arrived(k, g):
        pltpu.make_async_copy(hidden.at[k, g], hidden.at[k, g], recv_sem.at[k, g]).wait()

    def early(k, carry):
        arrived(k, near)
        convolve(k, 0, (near,))
        return carry

    def chunk(k, carry):
        arrived(k, far)
        convolve(k, 0, (far,))

        def section(s, carry):
            connect(k, s, False)
            convolve(k, s + 1, (0, 1))
            return carry

        lax.fori_loop(0, sections - 1, section, 0)
        connect(k, sections - 1, True)
        return carry

    early(0, 0)
    for (copy, first, count), target in zip(loads, (in_w, mid_w, out_w)):
        copy.wait()

        def other_split(n, carry, first=first, target=target):
            split_into(one_f32, first + n, target, n, 0, channels)
            return carry

        lax.fori_loop(0, count, other_split, 0)

    lax.fori_loop(1, chunks, early, 0)
    lax.fori_loop(0, chunks, chunk, 0)

    sent = x_ref.at[:, pl.ds(0, (devices - 1) * share)]
    pltpu.make_async_copy(sent, sent, send_sem).wait()
    pltpu.make_async_copy(sent, sent, back_send_sem).wait()
    pltpu.make_async_copy(y_ref, y_ref, back_recv_sem).wait()


def fused(
    mics,
    tms,
    signal,
    conv_weight,
    conv_bias,
    transform_in,
    transform_mid,
    transform_out,
    transform_offsets_bias,
):
    _, frames, channels = signal.shape
    sections, layers = conv_weight.shape[:2]
    half = frames // 2
    chunks = half // (mics * tms) // ROWS
    blocks = 2 * tms
    group = mics // 2
    rows = blocks * group * ROWS
    pad = 2 ** (layers - 1) * group * ROWS
    bf16, f32 = jnp.bfloat16, jnp.float32
    anywhere = pl.BlockSpec(memory_space=pl.ANY)
    out = pl.pallas_call(
        functools.partial(kernel, chunks, sections, layers),
        out_shape=pltpu.VMEM((2, half, channels), f32),
        in_specs=[anywhere] * 7,
        out_specs=pl.BlockSpec(memory_space=pltpu.VMEM),
        scratch_shapes=[
            pltpu.VMEM((chunks, 2, blocks, group, ROWS, channels), f32),
            pltpu.VMEM((2, pad + rows, 2 * channels), bf16),
            pltpu.VMEM((2, pad + rows, 2 * channels), bf16),
            pltpu.VMEM((2, rows, 2 * channels), bf16),
            pltpu.VMEM((sections * layers * 2, channels, channels), f32),
            pltpu.VMEM((sections * 4, channels, channels), f32),
            pltpu.VMEM((sections * layers, 4 * channels, channels), bf16),
            pltpu.VMEM((sections, 2 * channels, channels), bf16),
            pltpu.VMEM((sections, 2 * channels, channels), bf16),
            pltpu.VMEM((sections * 2, 2 * channels, channels), bf16),
            pltpu.VMEM((layers, sections, channels), f32),
            pltpu.VMEM((3, sections, channels), f32),
            pltpu.SemaphoreType.DMA,
            pltpu.SemaphoreType.DMA((chunks, 2)),
            pltpu.SemaphoreType.DMA,
            pltpu.SemaphoreType.DMA,
            pltpu.SemaphoreType.DMA((6,)),
        ],
        compiler_params=pltpu.CompilerParams(
            collective_id=0, has_side_effects=True, vmem_limit_bytes=60 * 1024 * 1024
        ),
        name="sections",
    )(
        signal.reshape(2, half, channels),
        conv_weight.reshape(-1, channels, channels),
        transform_in,
        transform_mid,
        transform_out.reshape(-1, channels, channels),
        conv_bias.swapaxes(0, 1),
        transform_offsets_bias.swapaxes(0, 1),
    )
    return out.reshape(1, frames, channels)


def solution(mesh):
    mics, tms = mesh.shape["mic"], mesh.shape["tm"]

    def run(signal, *parameters):
        half = signal.shape[1] // 2
        if half % (mics * tms * ROWS) == 0 and mics % 4 == 0:
            return fused(mics, tms, signal, *parameters)
        return body(signal, *parameters)

    placed = (P("mic", "tm", None), P(), P(), P(), P(), P(), P())
    return jax.shard_map(
        run, mesh=mesh, in_specs=placed, out_specs=P("mic", "tm", None), check_vma=False
    )
```

```python
import functools

import jax
import jax.numpy as jnp
from jax import lax
from jax.experimental import pallas as pl
from jax.experimental.pallas import tpu as pltpu
from jax.sharding import PartitionSpec as P

AXES = ("mic", "tm")
ROWS = 8
MESH = pl.DeviceIdType.MESH


def matmul(left, right):
    return jnp.dot(left, right, precision=lax.Precision.HIGH, preferred_element_type=jnp.float32)


def delay(values, steps):
    padding = jnp.zeros(values.shape[:1] + (steps,) + values.shape[2:], values.dtype)
    return jnp.concatenate([padding, values[:, : values.shape[1] - steps]], axis=1)


def body(
    signal,
    conv_weight,
    conv_bias,
    transform_in,
    transform_mid,
    transform_out,
    transform_offsets_bias,
):
    _, frames, channels = signal.shape
    sections, layers = conv_weight.shape[:2]
    half = frames // 2
    mics = lax.axis_size("mic")
    chains = lax.all_to_all(
        signal[0].reshape(2, half, channels), AXES, split_axis=1, concat_axis=0, tiled=True
    )
    hidden = chains.reshape(mics, -1, chains.shape[1], channels)
    for s in range(sections):
        for l in range(layers):
            delayed = delay(hidden, 2**l)
            hidden = hidden + jnp.tanh(
                matmul(hidden, conv_weight[s, l, 0])
                + matmul(delayed, conv_weight[s, l, 1])
                + conv_bias[s, l]
            )
        mapped = jnp.tanh(matmul(hidden, transform_in[s]) + transform_offsets_bias[s, 0])
        average = jnp.sum(mapped, axis=0) / jnp.float32(mics)
        pooled = jnp.tanh(matmul(average, transform_mid[s]) + transform_offsets_bias[s, 1])
        mixing = (
            matmul(mapped, transform_out[s, :channels])
            + matmul(pooled, transform_out[s, channels:])
            + transform_offsets_bias[s, 2]
        )
        hidden = hidden + jnp.tanh(mixing)
    back = lax.all_to_all(
        hidden.reshape(chains.shape), AXES, split_axis=0, concat_axis=1, tiled=True
    )
    return back.reshape(1, frames, channels)


def split(values):
    high = values.astype(jnp.bfloat16)
    return high, (values - high.astype(jnp.float32)).astype(jnp.bfloat16)


def dot(left, right):
    return jnp.dot(left, right, preferred_element_type=jnp.float32)


def kernel(
    chunks,
    sections,
    layers,
    x_ref,
    conv_hbm,
    in_hbm,
    mid_hbm,
    out_hbm,
    conv_bias_hbm,
    offsets_hbm,
    y_ref,
    hidden,
    act_a,
    act_b,
    act_u,
    conv_f32,
    one_f32,
    conv_w,
    in_w,
    mid_w,
    out_w,
    conv_bias,
    offsets,
    send_sem,
    recv_sem,
    back_send_sem,
    back_recv_sem,
    weight_sem,
):
    mics, tms = lax.axis_size("mic"), lax.axis_size("tm")
    devices = mics * tms
    my_mic, my_tm = lax.axis_index("mic"), lax.axis_index("tm")
    me = my_mic * tms + my_tm
    share = chunks * ROWS
    channels = x_ref.shape[2]
    blocks = 2 * tms
    rows = blocks * (mics // 2) * ROWS
    pad = act_a.shape[1] - rows

    group = mics // 2
    near = my_mic // group
    far = 1 - near
    my_place = lax.rem(my_mic, group)

    def send_each(act):
        for j in range(group):
            place = lax.rem(my_place + j, group)

            def one(jt, carry, place=place):
                t = lax.rem(my_tm + jt, tms)
                act(far, place, t)
                act(near, place, t)
                return carry

            if j == 0:
                act(far, place, my_tm)
            lax.fori_loop(1 if j == 0 else 0, tms, one, 0)

    bias_copies = [
        pltpu.make_async_copy(conv_bias_hbm, conv_bias, weight_sem.at[4]),
        pltpu.make_async_copy(offsets_hbm, offsets, weight_sem.at[5]),
    ]
    for copy in bias_copies:
        copy.start()
    barrier = pltpu.get_barrier_semaphore()
    send_each(
        lambda g, p, t: pl.semaphore_signal(
            barrier, inc=1, device_id=(g * group + p, t), device_id_type=MESH
        )
    )
    pl.semaphore_wait(barrier, devices - 1)

    def residues(owner, k):
        return pl.ds(pl.multiple_of(owner * share + k * ROWS, ROWS), ROWS)

    def send_chunk(k):
        def send(g, p, t):
            m = g * group + p
            pltpu.make_async_remote_copy(
                src_ref=x_ref.at[:, residues(m * tms + t, k)],
                dst_ref=hidden.at[k, near, pl.ds(2 * my_tm, 2), my_place],
                send_sem=send_sem,
                recv_sem=recv_sem.at[k, near],
                device_id=(m, t),
                device_id_type=MESH,
            ).start()

        send_each(send)
        pltpu.make_async_copy(
            x_ref.at[:, residues(me, k)],
            hidden.at[k, near, pl.ds(2 * my_tm, 2), my_place],
            recv_sem.at[k, near],
        ).start()

    send_chunk(0)

    conv_copy = pltpu.make_async_copy(conv_hbm, conv_f32, weight_sem.at[0])
    conv_copy.start()
    loads = []
    first = 0
    for n, source in enumerate((in_hbm, mid_hbm, out_hbm)):
        count = source.shape[0]
        copy = pltpu.make_async_copy(source, one_f32.at[pl.ds(first, count)], weight_sem.at[1 + n])
        copy.start()
        loads.append((copy, first, count))
        first += count
    for k in range(1, chunks):
        send_chunk(k)
    for g in range(2):
        act_a[g, pl.ds(0, pad), :] = jnp.zeros((pad, 2 * channels), jnp.bfloat16)
        act_b[g, pl.ds(0, pad), :] = jnp.zeros((pad, 2 * channels), jnp.bfloat16)

    step = 64

    def split_into(source, index, target, place, high_row, low_row):
        def part(i, carry):
            at = pl.multiple_of(i * step, step)
            high, low = split(source[index, pl.ds(at, step), :])
            target[place, pl.ds(pl.multiple_of(high_row + at, step), step), :] = high
            target[place, pl.ds(pl.multiple_of(low_row + at, step), step), :] = low
            return carry

        lax.fori_loop(0, channels // step, part, 0)

    for copy in bias_copies:
        copy.wait()
    conv_copy.wait()

    def conv_split(n, carry):
        for tap in range(2):
            split_into(conv_f32, 2 * n + tap, conv_w, n, tap * channels, (2 + tap) * channels)
        return carry

    lax.fori_loop(0, sections * layers, conv_split, 0)
    body = pl.ds(pad, rows)
    high_part, low_part = pl.ds(0, channels), pl.ds(channels, channels)
    shape = (blocks, group, ROWS, channels)

    def product(high, low, weight, n):
        return dot(jnp.concatenate([high, high], axis=1), weight[n]) + dot(
            low, weight[n, pl.ds(0, channels)]
        )

    def load(act, groups, part, columns):
        return jnp.concatenate([act[g, part, columns] for g in groups], axis=0)

    def store(act, g, part, values):
        high, low = split(values)
        act[g, part, high_part] = high
        act[g, part, low_part] = low

    def convolve(k, s, groups):
        for g in groups:
            store(act_a, g, body, hidden[k, g].reshape(rows, channels))
        here, there = act_a, act_b
        for l in range(layers):
            late = pl.ds(pad - 2**l * group * ROWS, rows)
            n = s * layers + l
            high = load(here, groups, body, high_part)
            late_high = load(here, groups, late, high_part)
            low = load(here, groups, body, low_part)
            late_low = load(here, groups, late, low_part)
            total = dot(
                jnp.concatenate([high, late_high, high, late_high], axis=1), conv_w[n]
            ) + dot(
                jnp.concatenate([low, late_low], axis=1),
                conv_w[n, pl.ds(0, 2 * channels)],
            )
            delta = jnp.tanh(total + conv_bias[l, pl.ds(s, 1), :])
            for i, g in enumerate(groups):
                new = hidden[k, g] + delta[i * rows : (i + 1) * rows].reshape(shape)
                hidden[k, g] = new
                if l < layers - 1:
                    store(there, g, body, new.reshape(rows, channels))
            here, there = there, here

    def connect(k, s):
        high, low = split(hidden[k].reshape(2 * rows, channels))
        mapped = jnp.tanh(product(high, low, in_w, s) + offsets[0, pl.ds(s, 1), :])
        for g in range(2):
            store(act_u, g, pl.ds(0, rows), mapped[g * rows : (g + 1) * rows])
        average = jnp.sum(mapped.reshape((2,) + shape), axis=(0, 2)) / jnp.float32(mics)
        high, low = split(average.reshape(blocks * ROWS, channels))
        pooled = jnp.tanh(product(high, low, mid_w, s) + offsets[1, pl.ds(s, 1), :])
        high, low = split(pooled)
        shared = product(high, low, out_w, 2 * s + 1) + offsets[2, pl.ds(s, 1), :]
        shared = shared.reshape(blocks, 1, ROWS, channels)
        high = load(act_u, (0, 1), pl.ds(0, rows), high_part)
        low = load(act_u, (0, 1), pl.ds(0, rows), low_part)
        mixing = product(high, low, out_w, 2 * s).reshape((2,) + shape)
        hidden[k] = hidden[k] + jnp.tanh(mixing + shared)

    def send_back(k):
        def send(g, p, t):
            pltpu.make_async_remote_copy(
                src_ref=hidden.at[k, g, pl.ds(2 * t, 2), p],
                dst_ref=y_ref.at[:, residues(me, k)],
                send_sem=back_send_sem,
                recv_sem=back_recv_sem,
                device_id=(g * group + p, t),
                device_id_type=MESH,
            ).start()

        send_each(send)
        pltpu.make_async_copy(
            hidden.at[k, near, pl.ds(2 * my_tm, 2), my_place],
            y_ref.at[:, residues(me, k)],
            back_recv_sem,
        ).start()

    def arrived(k, g):
        pltpu.make_async_copy(hidden.at[k, g], hidden.at[k, g], recv_sem.at[k, g]).wait()

    def early(k, carry):
        arrived(k, near)
        convolve(k, 0, (near,))
        return carry

    def chunk(k, carry):
        arrived(k, far)
        convolve(k, 0, (far,))

        def section(s, carry):
            connect(k, s)
            convolve(k, s + 1, (0, 1))
            return carry

        lax.fori_loop(0, sections - 1, section, 0)
        connect(k, sections - 1)
        send_back(k)
        return carry

    early(0, 0)
    for (copy, first, count), target in zip(loads, (in_w, mid_w, out_w)):
        copy.wait()

        def other_split(n, carry, first=first, target=target):
            split_into(one_f32, first + n, target, n, 0, channels)
            return carry

        lax.fori_loop(0, count, other_split, 0)

    lax.fori_loop(1, chunks, early, 0)
    lax.fori_loop(0, chunks, chunk, 0)

    sent = x_ref.at[:, pl.ds(0, (devices - 1) * share)]
    pltpu.make_async_copy(sent, sent, send_sem).wait()
    pltpu.make_async_copy(sent, sent, back_send_sem).wait()
    pltpu.make_async_copy(y_ref, y_ref, back_recv_sem).wait()


def fused(
    mics,
    tms,
    signal,
    conv_weight,
    conv_bias,
    transform_in,
    transform_mid,
    transform_out,
    transform_offsets_bias,
):
    _, frames, channels = signal.shape
    sections, layers = conv_weight.shape[:2]
    half = frames // 2
    chunks = half // (mics * tms) // ROWS
    blocks = 2 * tms
    group = mics // 2
    rows = blocks * group * ROWS
    pad = 2 ** (layers - 1) * group * ROWS
    bf16, f32 = jnp.bfloat16, jnp.float32
    anywhere = pl.BlockSpec(memory_space=pl.ANY)
    out = pl.pallas_call(
        functools.partial(kernel, chunks, sections, layers),
        out_shape=pltpu.VMEM((2, half, channels), f32),
        in_specs=[anywhere] * 7,
        out_specs=pl.BlockSpec(memory_space=pltpu.VMEM),
        scratch_shapes=[
            pltpu.VMEM((chunks, 2, blocks, group, ROWS, channels), f32),
            pltpu.VMEM((2, pad + rows, 2 * channels), bf16),
            pltpu.VMEM((2, pad + rows, 2 * channels), bf16),
            pltpu.VMEM((2, rows, 2 * channels), bf16),
            pltpu.VMEM((sections * layers * 2, channels, channels), f32),
            pltpu.VMEM((sections * 4, channels, channels), f32),
            pltpu.VMEM((sections * layers, 4 * channels, channels), bf16),
            pltpu.VMEM((sections, 2 * channels, channels), bf16),
            pltpu.VMEM((sections, 2 * channels, channels), bf16),
            pltpu.VMEM((sections * 2, 2 * channels, channels), bf16),
            pltpu.VMEM((layers, sections, channels), f32),
            pltpu.VMEM((3, sections, channels), f32),
            pltpu.SemaphoreType.DMA,
            pltpu.SemaphoreType.DMA((chunks, 2)),
            pltpu.SemaphoreType.DMA,
            pltpu.SemaphoreType.DMA,
            pltpu.SemaphoreType.DMA((6,)),
        ],
        compiler_params=pltpu.CompilerParams(
            collective_id=0, has_side_effects=True, vmem_limit_bytes=60 * 1024 * 1024
        ),
        name="sections",
    )(
        signal.reshape(2, half, channels),
        conv_weight.reshape(-1, channels, channels),
        transform_in,
        transform_mid,
        transform_out.reshape(-1, channels, channels),
        conv_bias.swapaxes(0, 1),
        transform_offsets_bias.swapaxes(0, 1),
    )
    return out.reshape(1, frames, channels)


def solution(mesh):
    mics, tms = mesh.shape["mic"], mesh.shape["tm"]

    def run(signal, *parameters):
        half = signal.shape[1] // 2
        if half % (mics * tms * ROWS) == 0 and mics % 4 == 0:
            return fused(mics, tms, signal, *parameters)
        return body(signal, *parameters)

    placed = (P("mic", "tm", None), P(), P(), P(), P(), P(), P())
    return jax.shard_map(
        run, mesh=mesh, in_specs=placed, out_specs=P("mic", "tm", None), check_vma=False
    )
```

```python
import functools

import jax
import jax.numpy as jnp
from jax import lax
from jax.experimental import pallas as pl
from jax.experimental.pallas import tpu as pltpu
from jax.sharding import PartitionSpec as P

AXES = ("mic", "tm")
ROWS = 8
MESH = pl.DeviceIdType.MESH


def matmul(left, right):
    return jnp.dot(left, right, precision=lax.Precision.HIGH, preferred_element_type=jnp.float32)


def delay(values, steps):
    padding = jnp.zeros(values.shape[:1] + (steps,) + values.shape[2:], values.dtype)
    return jnp.concatenate([padding, values[:, : values.shape[1] - steps]], axis=1)


def body(
    signal,
    conv_weight,
    conv_bias,
    transform_in,
    transform_mid,
    transform_out,
    transform_offsets_bias,
):
    _, frames, channels = signal.shape
    sections, layers = conv_weight.shape[:2]
    half = frames // 2
    mics = lax.axis_size("mic")
    chains = lax.all_to_all(
        signal[0].reshape(2, half, channels), AXES, split_axis=1, concat_axis=0, tiled=True
    )
    hidden = chains.reshape(mics, -1, chains.shape[1], channels)
    for s in range(sections):
        for l in range(layers):
            delayed = delay(hidden, 2**l)
            hidden = hidden + jnp.tanh(
                matmul(hidden, conv_weight[s, l, 0])
                + matmul(delayed, conv_weight[s, l, 1])
                + conv_bias[s, l]
            )
        mapped = jnp.tanh(matmul(hidden, transform_in[s]) + transform_offsets_bias[s, 0])
        average = jnp.sum(mapped, axis=0) / jnp.float32(mics)
        pooled = jnp.tanh(matmul(average, transform_mid[s]) + transform_offsets_bias[s, 1])
        mixing = (
            matmul(mapped, transform_out[s, :channels])
            + matmul(pooled, transform_out[s, channels:])
            + transform_offsets_bias[s, 2]
        )
        hidden = hidden + jnp.tanh(mixing)
    back = lax.all_to_all(
        hidden.reshape(chains.shape), AXES, split_axis=0, concat_axis=1, tiled=True
    )
    return back.reshape(1, frames, channels)


def split(values):
    high = values.astype(jnp.bfloat16)
    return high, (values - high.astype(jnp.float32)).astype(jnp.bfloat16)


def dot(left, right):
    return jnp.dot(left, right, preferred_element_type=jnp.float32)


def kernel(
    chunks,
    sections,
    layers,
    x_ref,
    conv_hbm,
    in_hbm,
    mid_hbm,
    out_hbm,
    conv_bias_hbm,
    offsets_hbm,
    y_ref,
    hidden,
    act_a,
    act_b,
    act_u,
    conv_f32,
    one_f32,
    conv_w,
    in_w,
    mid_w,
    out_w,
    conv_bias,
    offsets,
    send_sem,
    recv_sem,
    back_send_sem,
    back_recv_sem,
    weight_sem,
):
    mics, tms = lax.axis_size("mic"), lax.axis_size("tm")
    devices = mics * tms
    my_mic, my_tm = lax.axis_index("mic"), lax.axis_index("tm")
    me = my_mic * tms + my_tm
    share = chunks * ROWS
    channels = x_ref.shape[2]
    blocks = 2 * tms
    rows = blocks * (mics // 2) * ROWS
    pad = act_a.shape[1] - rows

    group = mics // 2
    near = my_mic // group
    far = 1 - near
    my_place = lax.rem(my_mic, group)

    def send_each(act):
        for j in range(group):
            place = lax.rem(my_place + j, group)

            def one(jt, carry, place=place):
                t = lax.rem(my_tm + jt, tms)
                act(far, place, t)
                act(near, place, t)
                return carry

            if j == 0:
                act(far, place, my_tm)
            lax.fori_loop(1 if j == 0 else 0, tms, one, 0)

    bias_copies = [
        pltpu.make_async_copy(conv_bias_hbm, conv_bias, weight_sem.at[4]),
        pltpu.make_async_copy(offsets_hbm, offsets, weight_sem.at[5]),
    ]
    for copy in bias_copies:
        copy.start()
    barrier = pltpu.get_barrier_semaphore()
    send_each(
        lambda g, p, t: pl.semaphore_signal(
            barrier, inc=1, device_id=(g * group + p, t), device_id_type=MESH
        )
    )
    pl.semaphore_wait(barrier, devices - 1)

    def residues(owner, k):
        return pl.ds(pl.multiple_of(owner * share + k * ROWS, ROWS), ROWS)

    def send_chunk(k):
        def send(g, p, t):
            m = g * group + p
            pltpu.make_async_remote_copy(
                src_ref=x_ref.at[:, residues(m * tms + t, k)],
                dst_ref=hidden.at[k, near, pl.ds(2 * my_tm, 2), my_place],
                send_sem=send_sem,
                recv_sem=recv_sem.at[k, near],
                device_id=(m, t),
                device_id_type=MESH,
            ).start()

        send_each(send)
        pltpu.make_async_copy(
            x_ref.at[:, residues(me, k)],
            hidden.at[k, near, pl.ds(2 * my_tm, 2), my_place],
            recv_sem.at[k, near],
        ).start()

    send_chunk(0)

    conv_copy = pltpu.make_async_copy(conv_hbm, conv_f32, weight_sem.at[0])
    conv_copy.start()
    loads = []
    first = 0
    for n, source in enumerate((in_hbm, mid_hbm, out_hbm)):
        count = source.shape[0]
        copy = pltpu.make_async_copy(source, one_f32.at[pl.ds(first, count)], weight_sem.at[1 + n])
        copy.start()
        loads.append((copy, first, count))
        first += count
    for g in range(2):
        act_a[g, pl.ds(0, pad), :] = jnp.zeros((pad, 2 * channels), jnp.bfloat16)
        act_b[g, pl.ds(0, pad), :] = jnp.zeros((pad, 2 * channels), jnp.bfloat16)

    step = 64

    def split_into(source, index, target, place, high_row, low_row):
        def part(i, carry):
            at = pl.multiple_of(i * step, step)
            high, low = split(source[index, pl.ds(at, step), :])
            target[place, pl.ds(pl.multiple_of(high_row + at, step), step), :] = high
            target[place, pl.ds(pl.multiple_of(low_row + at, step), step), :] = low
            return carry

        lax.fori_loop(0, channels // step, part, 0)

    for copy in bias_copies:
        copy.wait()
    conv_copy.wait()

    def conv_split(n, carry):
        for tap in range(2):
            split_into(conv_f32, 2 * n + tap, conv_w, n, tap * channels, (2 + tap) * channels)
        return carry

    lax.fori_loop(0, sections * layers, conv_split, 0)
    body = pl.ds(pad, rows)
    high_part, low_part = pl.ds(0, channels), pl.ds(channels, channels)
    shape = (blocks, group, ROWS, channels)

    def product(high, low, weight, n):
        return dot(jnp.concatenate([high, high], axis=1), weight[n]) + dot(
            low, weight[n, pl.ds(0, channels)]
        )

    def load(act, groups, part, columns):
        return jnp.concatenate([act[g, part, columns] for g in groups], axis=0)

    def store(act, g, part, values):
        high, low = split(values)
        act[g, part, high_part] = high
        act[g, part, low_part] = low

    def convolve(k, s, groups):
        for g in groups:
            store(act_a, g, body, hidden[k, g].reshape(rows, channels))
        here, there = act_a, act_b
        for l in range(layers):
            late = pl.ds(pad - 2**l * group * ROWS, rows)
            n = s * layers + l
            high = load(here, groups, body, high_part)
            late_high = load(here, groups, late, high_part)
            low = load(here, groups, body, low_part)
            late_low = load(here, groups, late, low_part)
            total = dot(
                jnp.concatenate([high, late_high, high, late_high], axis=1), conv_w[n]
            ) + dot(
                jnp.concatenate([low, late_low], axis=1),
                conv_w[n, pl.ds(0, 2 * channels)],
            )
            delta = jnp.tanh(total + conv_bias[l, pl.ds(s, 1), :])
            for i, g in enumerate(groups):
                new = hidden[k, g] + delta[i * rows : (i + 1) * rows].reshape(shape)
                hidden[k, g] = new
                if l < layers - 1:
                    store(there, g, body, new.reshape(rows, channels))
            here, there = there, here

    def connect(k, s):
        high, low = split(hidden[k].reshape(2 * rows, channels))
        mapped = jnp.tanh(product(high, low, in_w, s) + offsets[0, pl.ds(s, 1), :])
        for g in range(2):
            store(act_u, g, pl.ds(0, rows), mapped[g * rows : (g + 1) * rows])
        average = jnp.sum(mapped.reshape((2,) + shape), axis=(0, 2)) / jnp.float32(mics)
        high, low = split(average.reshape(blocks * ROWS, channels))
        pooled = jnp.tanh(product(high, low, mid_w, s) + offsets[1, pl.ds(s, 1), :])
        high, low = split(pooled)
        shared = product(high, low, out_w, 2 * s + 1) + offsets[2, pl.ds(s, 1), :]
        shared = shared.reshape(blocks, 1, ROWS, channels)
        high = load(act_u, (0, 1), pl.ds(0, rows), high_part)
        low = load(act_u, (0, 1), pl.ds(0, rows), low_part)
        mixing = product(high, low, out_w, 2 * s).reshape((2,) + shape)
        hidden[k] = hidden[k] + jnp.tanh(mixing + shared)

    def send_back(k):
        def send(g, p, t):
            pltpu.make_async_remote_copy(
                src_ref=hidden.at[k, g, pl.ds(2 * t, 2), p],
                dst_ref=y_ref.at[:, residues(me, k)],
                send_sem=back_send_sem,
                recv_sem=back_recv_sem,
                device_id=(g * group + p, t),
                device_id_type=MESH,
            ).start()

        send_each(send)
        pltpu.make_async_copy(
            hidden.at[k, near, pl.ds(2 * my_tm, 2), my_place],
            y_ref.at[:, residues(me, k)],
            back_recv_sem,
        ).start()

    def arrived(k, g):
        pltpu.make_async_copy(hidden.at[k, g], hidden.at[k, g], recv_sem.at[k, g]).wait()

    def early(k, carry):
        arrived(k, near)
        convolve(k, 0, (near,))
        return carry

    def chunk(k, carry):
        arrived(k, far)
        convolve(k, 0, (far,))

        def section(s, carry):
            connect(k, s)
            convolve(k, s + 1, (0, 1))
            return carry

        lax.fori_loop(0, sections - 1, section, 0)
        connect(k, sections - 1)
        send_back(k)
        return carry

    for k in range(1, chunks):
        send_chunk(k)
    early(0, 0)
    for (copy, first, count), target in zip(loads, (in_w, mid_w, out_w)):
        copy.wait()

        def other_split(n, carry, first=first, target=target):
            split_into(one_f32, first + n, target, n, 0, channels)
            return carry

        lax.fori_loop(0, count, other_split, 0)

    lax.fori_loop(1, chunks, early, 0)
    lax.fori_loop(0, chunks, chunk, 0)

    sent = x_ref.at[:, pl.ds(0, (devices - 1) * share)]
    pltpu.make_async_copy(sent, sent, send_sem).wait()
    pltpu.make_async_copy(sent, sent, back_send_sem).wait()
    pltpu.make_async_copy(y_ref, y_ref, back_recv_sem).wait()


def fused(
    mics,
    tms,
    signal,
    conv_weight,
    conv_bias,
    transform_in,
    transform_mid,
    transform_out,
    transform_offsets_bias,
):
    _, frames, channels = signal.shape
    sections, layers = conv_weight.shape[:2]
    half = frames // 2
    chunks = half // (mics * tms) // ROWS
    blocks = 2 * tms
    group = mics // 2
    rows = blocks * group * ROWS
    pad = 2 ** (layers - 1) * group * ROWS
    bf16, f32 = jnp.bfloat16, jnp.float32
    anywhere = pl.BlockSpec(memory_space=pl.ANY)
    out = pl.pallas_call(
        functools.partial(kernel, chunks, sections, layers),
        out_shape=pltpu.VMEM((2, half, channels), f32),
        in_specs=[anywhere] * 7,
        out_specs=pl.BlockSpec(memory_space=pltpu.VMEM),
        scratch_shapes=[
            pltpu.VMEM((chunks, 2, blocks, group, ROWS, channels), f32),
            pltpu.VMEM((2, pad + rows, 2 * channels), bf16),
            pltpu.VMEM((2, pad + rows, 2 * channels), bf16),
            pltpu.VMEM((2, rows, 2 * channels), bf16),
            pltpu.VMEM((sections * layers * 2, channels, channels), f32),
            pltpu.VMEM((sections * 4, channels, channels), f32),
            pltpu.VMEM((sections * layers, 4 * channels, channels), bf16),
            pltpu.VMEM((sections, 2 * channels, channels), bf16),
            pltpu.VMEM((sections, 2 * channels, channels), bf16),
            pltpu.VMEM((sections * 2, 2 * channels, channels), bf16),
            pltpu.VMEM((layers, sections, channels), f32),
            pltpu.VMEM((3, sections, channels), f32),
            pltpu.SemaphoreType.DMA,
            pltpu.SemaphoreType.DMA((chunks, 2)),
            pltpu.SemaphoreType.DMA,
            pltpu.SemaphoreType.DMA,
            pltpu.SemaphoreType.DMA((6,)),
        ],
        compiler_params=pltpu.CompilerParams(
            collective_id=0, has_side_effects=True, vmem_limit_bytes=60 * 1024 * 1024
        ),
        name="sections",
    )(
        signal.reshape(2, half, channels),
        conv_weight.reshape(-1, channels, channels),
        transform_in,
        transform_mid,
        transform_out.reshape(-1, channels, channels),
        conv_bias.swapaxes(0, 1),
        transform_offsets_bias.swapaxes(0, 1),
    )
    return out.reshape(1, frames, channels)


def solution(mesh):
    mics, tms = mesh.shape["mic"], mesh.shape["tm"]

    def run(signal, *parameters):
        half = signal.shape[1] // 2
        if half % (mics * tms * ROWS) == 0 and mics % 4 == 0:
            return fused(mics, tms, signal, *parameters)
        return body(signal, *parameters)

    placed = (P("mic", "tm", None), P(), P(), P(), P(), P(), P())
    return jax.shard_map(
        run, mesh=mesh, in_specs=placed, out_specs=P("mic", "tm", None), check_vma=False
    )
```
